32 devices in a mesh: state: 2 (over x), wide: 16 (over z, y, core).
Axes of the slice: x: 2, y: 2, z: 4, core: 2. Of those that a mesh axis runs over, the one named last changes fastest.
Arguments:
- block_answers: float32 [32768, 512], P(('state', 'wide')), parts along dimension 0, may hold values from -24 to 24
- block_owner: int32 [32768, 1], P(('state', 'wide')), parts along dimension 0, may hold values from 0 to 15; in each aligned block of 1024 rows (0 to 1023, 1024 to 2047, ...) at most 80 rows name the same one
- block_place: int32 [32768], P(('state', 'wide')), parts along dimension 0, may hold values from 0 to 63
- tract_answers: float32 [2048, 512], P(('state', 'wide')), parts along dimension 0, may hold values from -24 to 24
- tract_county: int32 [2048], P(('state', 'wide')), parts along dimension 0, may hold values from 0 to 87
- county_answers: float32 [176, 512], P('state'), parts along dimension 0, may hold values from -24 to 24
- state_answers: float32 [2, 512], P('state'), parts along dimension 0, may hold values from -24 to 24
- query_members: int32 [2016, 8], replicated, may hold values from 0 to 511, all different within a row
- query_precision: float32 [4, 512], replicated, may hold values from 0.25 to 4
Outputs:
- block_histogram: float32 [32768, 2016], P(('state', 'wide')), parts along dimension 0
- tract_histogram: float32 [2048, 2016], P(('state', 'wide')), parts along dimension 0
- county_histogram: float32 [176, 2016], P('state'), parts along dimension 0
The draws below stay inside these ranges and needn't reach their ends.
There are 2 independent parts, one for each index of `state`. The reference program is written for one: setup_inputs(seed, part) draws one part's arguments, and reference() takes and returns one part's arrays. A program takes and returns all parts, laid end to end along the dimension named above; an argument that names none is the same for every part. Nothing has to cross between parts.
Inputs may be any that keep to these rules, and one draw needn't show every extreme that they name: `block_owner`: in each aligned block of 1024 rows (the blocks of one device) no owner is named by more than 80 rows. `query_members`: each row names 8 different queries, and every query is named by some row.
All inputs are finite; a program needn't handle non-finite values.
Results may differ from the reference program's by a relative error of at most 0.00005.
Values sent between devices are 32-bit elements; how exact they have to be, the bound alone decides.
A program may use at most 128 MiB of HBM per device.

```python
import math
import jax
import jax.numpy as jnp
import numpy as np
from jax import lax

CELLS = 2016
NQ = 512
MEMBERS = 8
LEVELS = 4
COUNTIES = 88
BLK_DEV = 1024
TR_DEV = 64
CAP = 80
BLOCKS = 16384
TRACTS = 1024
N_WIDE = 16


def touch_ends(result, rng, low, top_value):
    dims = result.shape
    spot = [jax.random.randint(jax.random.fold_in(rng, axis), (), 0, dims[axis]) for axis in range(len(dims))]
    result = result.at[tuple(spot)].set(low)
    longest = dims.index(max(dims))
    spot[longest] = (spot[longest] + 1) % dims[longest]
    return result.at[tuple(spot)].set(top_value)


def shard_levels(own_key, extent, shards, smallest, top_value):
    loudness, own = 1.0, jax.random.fold_in(own_key, 6)
    for position, blocks in shards:
        steps = jnp.exp(jax.random.uniform(jax.random.fold_in(own, position), (blocks,), jnp.float32, smallest / len(shards), top_value / len(shards)))
        loudness = loudness * jnp.repeat(steps, extent[position] // blocks).reshape([-1 if axis == position else 1 for axis in range(len(extent))])
    return loudness


def choose_distinct(own_key, rows, number_of, top, lift):
    ranking = jax.random.permutation(jax.random.fold_in(own_key, 1), number_of)
    favour = ranking
    for power in range(3):
        favour = favour * favour // number_of
    favour = favour * lift // number_of
    lots = jax.random.randint(jax.random.fold_in(own_key, 2), (rows, number_of), 0, 4096) + favour
    holders = jax.random.permutation(jax.random.fold_in(own_key, 3), rows)[jnp.arange(number_of) % rows]
    lots = jnp.where(jnp.arange(rows)[:, None] == holders[None, :], 1 << 14, lots)
    score = lots * number_of + jnp.arange(number_of)
    return lax.top_k(score.astype(jnp.int32), top)[1].astype(jnp.int32)


def deal_out(stream_key, own, number, rows, number_of, top, most, lean):
    order = jax.random.permutation(stream_key, number_of)
    packed, usual = portions_of(number_of, rows * top, most, lean, True), portions_of(number_of, rows * top, most, lean, False)
    places = jnp.arange(number_of)

    def named(sizes, rotation):
        used = int((sizes > 0).sum())
        fixed = max(1, used // 4)
        shifted = fixed + (places - fixed + rotation * (used - fixed)) % max(1, number_of - fixed)
        return jnp.zeros((number_of,), jnp.int32).at[order[jnp.where(places < fixed, places, shifted)]].set(jnp.asarray(sizes, jnp.int32))

    sizes = jnp.where(number % 4 == 0, named(packed, number // 4), named(usual, number - number // 4 - 1))
    mixed = jax.random.permutation(jax.random.fold_in(own, 3), number_of)
    source_of, receiver = mixed[0:number_of // 2 * 2:2], mixed[1:number_of // 2 * 2:2]
    margin = jnp.minimum(sizes[source_of] - 1, most - sizes[receiver]) // 2
    margin = jnp.where((source_of == order[0]) | (receiver == order[0]) | (sizes[receiver] == 0), 0, jnp.maximum(margin, 0))
    shifted = jax.random.randint(jax.random.fold_in(own, 4), (number_of // 2,), 0, 1 << 20) % (margin + 1)
    sizes = sizes.at[source_of].add(-shifted).at[receiver].add(shifted)
    items = jnp.searchsorted(jnp.cumsum(sizes), jnp.arange(rows * top), side="right").astype(jnp.int32)
    table = items.reshape(top, rows).T
    table = table[jax.random.permutation(jax.random.fold_in(own, 1), rows)]
    rotation = jax.random.randint(jax.random.fold_in(own, 2), (rows, 1), 0, top)
    return jnp.take_along_axis(table, (jnp.arange(top)[None, :] + rotation) % top, axis=1)


def portions_of(number_of, total, limit, lean, full):
    weights = [(1 << 20) // math.isqrt(grade ** lean) + 1 for grade in range(1, number_of + 1)]
    largest = limit if full else min(limit, max(-(-total // number_of), total * weights[0] // sum(weights)))
    least = 1 if total - largest >= number_of - 1 else 0
    given, surplus = [largest] + [least] * (number_of - 1), total - largest - least * (number_of - 1)
    while surplus > 0:
        free = [i for i in range(1, number_of) if given[i] < largest] or [i for i in range(1, number_of) if given[i] < limit]
        pool, remaining = sum([weights[i] for i in free]), surplus
        for i in free:
            extra = min(limit - given[i], max(1, remaining * weights[i] // pool), surplus)
            given[i] = given[i] + extra
            surplus = surplus - extra
    return np.array(given)


def centred(stream_key, extent, spread, limit, shards=(), kind=jnp.bfloat16):
    drawn = spread * jax.random.normal(stream_key, extent, jnp.float32)
    if shards:
        drawn = drawn * shard_levels(stream_key, extent, shards, -0.22, 0.18)
    return jnp.clip(drawn, -limit, limit).astype(kind)


def setup_inputs(seed: int = 0, part: int = 0) -> dict:
    key_of = jax.random.split(jax.random.key(seed), 10)
    part_splits = jax.random.split(jax.random.fold_in(key_of[9], part), 10)
    block_answers = centred(part_splits[0], (BLOCKS, NQ), 4.0, 24.0, ((0, 16),), jnp.float32)
    block_owner_keys = jax.random.split(jax.random.fold_in(part_splits[1], 1), BLOCKS // BLK_DEV)
    block_owner_turns = jax.random.permutation(jax.random.fold_in(part_splits[1], 3), BLOCKS // BLK_DEV)
    block_owner = jax.vmap(lambda own, number: deal_out(jax.random.fold_in(part_splits[1], 2), own, number, BLK_DEV, N_WIDE, 1, CAP, 1))(block_owner_keys, block_owner_turns).reshape((BLOCKS, 1))
    block_place = touch_ends(jax.random.randint(part_splits[2], (BLOCKS,), 0, TR_DEV), jax.random.fold_in(part_splits[2], 1), 0, TR_DEV - 1).astype(jnp.int32)
    tract_answers = centred(part_splits[3], (TRACTS, NQ), 4.0, 24.0, ((0, 16),), jnp.float32)
    tract_county = touch_ends(jax.random.randint(part_splits[4], (TRACTS,), 0, COUNTIES), jax.random.fold_in(part_splits[4], 1), 0, COUNTIES - 1).astype(jnp.int32)
    county_answers = centred(part_splits[5], (COUNTIES, NQ), 4.0, 24.0, (), jnp.float32)
    state_answers = centred(part_splits[6], (1, NQ), 4.0, 24.0, (), jnp.float32)
    query_members = choose_distinct(key_of[7], CELLS, NQ, MEMBERS, 0)
    query_precision = jnp.clip(jnp.exp(jax.random.uniform(key_of[8], (LEVELS, NQ), jnp.float32, math.log(0.25), math.log(4.0))), 0.25, 4.0)
    return dict(block_answers=block_answers, block_owner=block_owner, block_place=block_place, tract_answers=tract_answers, tract_county=tract_county, county_answers=county_answers, state_answers=state_answers, query_members=query_members, query_precision=query_precision)


FULL_PRECISION = lax.Precision.HIGHEST


def cover_matrix(query_members, queries):
    labels = jnp.arange(queries, dtype=jnp.int32)
    covered = jnp.zeros((queries, query_members.shape[0]), jnp.float32)
    for member in range(query_members.shape[1]):
        covered = covered + (labels[:, None] == query_members[None, :, member]).astype(jnp.float32)
    return covered


def estimate(answers, weights, cover_table, coverage):
    weighted = answers * weights[None, :]
    return jnp.dot(weighted, cover_table, precision=FULL_PRECISION, preferred_element_type=jnp.float32) / coverage[None, :]


def reference(block_answers, block_owner, block_place, tract_answers, tract_county, county_answers, state_answers, query_members, query_precision):
    cover_table = cover_matrix(query_members, NQ)
    coverage = jnp.dot(query_precision, cover_table, precision=FULL_PRECISION, preferred_element_type=jnp.float32)
    variance = 1.0 / coverage
    block_measured = estimate(block_answers, query_precision[0], cover_table, coverage[0])
    tract_measured = estimate(tract_answers, query_precision[1], cover_table, coverage[1])
    county_measured = estimate(county_answers, query_precision[2], cover_table, coverage[2])
    state_measured = estimate(state_answers, query_precision[3], cover_table, coverage[3])
    tract_of = (block_owner[:, 0] * TR_DEV + block_place).astype(jnp.int32)
    child_sum = jax.ops.segment_sum(block_measured, tract_of, num_segments=TRACTS)
    child_count = jax.ops.segment_sum(jnp.ones((BLOCKS,), jnp.float32), tract_of, num_segments=TRACTS)
    child_spread = child_count[:, None] * variance[0][None, :]
    tract_total = child_spread + variance[1][None, :]
    tract_joined = (child_spread * tract_measured + variance[1][None, :] * child_sum) / tract_total
    tract_spread = child_spread * variance[1][None, :] / tract_total
    county_child = jax.ops.segment_sum(tract_joined, tract_county, num_segments=COUNTIES)
    county_child_spread = jax.ops.segment_sum(tract_spread, tract_county, num_segments=COUNTIES)
    county_total = county_child_spread + variance[2][None, :]
    county_joined = (county_child_spread * county_measured + variance[2][None, :] * county_child) / county_total
    county_spread = county_child_spread * variance[2][None, :] / county_total
    state_sum = jnp.sum(county_joined, axis=0, keepdims=True)
    state_spread = jnp.sum(county_spread, axis=0, keepdims=True)
    state_rate = (state_measured - state_sum) / (state_spread + variance[3][None, :])
    county_rate = (county_measured - county_child + variance[2][None, :] * state_rate) / county_total
    county_histogram = county_joined + county_spread * state_rate
    above = county_rate[tract_county]
    tract_rate = (tract_measured - child_sum + variance[1][None, :] * above) / tract_total
    tract_histogram = tract_joined + tract_spread * above
    block_histogram = block_measured + variance[0][None, :] * tract_rate[tract_of]
    return (block_histogram, tract_histogram, county_histogram)
```

```python
import functools
import itertools

import jax
import jax.numpy as jnp
from jax import lax
from jax.experimental import pallas as pl
from jax.experimental.pallas import tpu as pltpu
from jax.sharding import PartitionSpec as P

LANES = 128
CHUNKS = 16
MESH = pl.DeviceIdType.MESH
F32 = jnp.float32
BF16 = jnp.bfloat16


def halves(x):
    high = x.astype(BF16)
    return high, (x - high.astype(F32)).astype(BF16)


def product(left, right):
    return jnp.dot(left, right, preferred_element_type=F32)


def two_products(high, low, right):
    return product(high, right) + product(low, right)


def picked(table, row_of):
    groups = table.shape[0]
    count = row_of.shape[0]
    wide = jnp.zeros((count, LANES), F32)
    for g in range(groups):
        wide = jnp.where(row_of // LANES == g, table[g : g + 1, :], wide)
    lane = lax.broadcasted_iota(jnp.int32, (count, LANES), 1)
    return jnp.sum(jnp.where(lane == row_of % LANES, wide, 0.0), axis=1, keepdims=True)


def tree_kernel(
    n,
    ba_ref,
    tof_row_ref,
    tof_col_ref,
    ta_ref,
    tc_ref,
    cs_ref,
    mt_ref,
    qp_ref,
    g1h_ref,
    g1l_ref,
    gsh_ref,
    gsl_ref,
    cover_ref,
    var_ref,
    tab_ref,
    rate_ref,
    hist_ref,
    acc,
    g1,
    gs,
    g2,
    misc,
    misc_send,
    misc_recv,
    send_sems,
    recv_sems,
    *rbufs,
):
    nb = n.bit_length() - 1
    me = lax.axis_index("wide")
    rows, queries = ta_ref.shape
    blocks = ba_ref.shape[0]
    cells = cover_ref.shape[1]
    groups = n * rows // LANES
    counties = rate_ref.shape[0]
    half = queries // 2
    bit = [(me // (1 << b)) % 2 for b in range(nb)]
    orders = [list(range(nb)), [0] + list(range(2, nb)) + [1]]
    cols = [pl.ds(0, half), pl.ds(half, half)]
    used = [0]
    sends = []

    def partner(b):
        return me + (1 - 2 * bit[b]) * (1 << b)

    def remote(src, dst, b):
        k = used[0]
        used[0] += 1
        copy = pltpu.make_async_remote_copy(
            src_ref=src,
            dst_ref=dst,
            send_sem=send_sems.at[k],
            recv_sem=recv_sems.at[k],
            device_id={"wide": partner(b)},
            device_id_type=MESH,
        )
        copy.start()
        sends.append(copy)
        return copy

    def at(values, low=0):
        return tuple(values[b] for b in range(nb - 1, low - 1, -1))

    def scatter_start(g, k):
        order = orders[g]
        values = [slice(None)] * nb
        for b in order[:k]:
            values[b] = bit[b]
        values[order[k]] = 1 - bit[order[k]]
        src = acc.at[at(values) + (slice(None), cols[g])]
        return remote(src, rbufs[g * nb + k], order[k])

    def scatter_add(g, k):
        order = orders[g]
        rest = sorted(order[k + 1 :], reverse=True)
        for combo in itertools.product((0, 1), repeat=len(rest)):
            values = list(bit)
            for b, v in zip(rest, combo):
                values[b] = v
            spot = at(values) + (slice(None), cols[g])
            acc[spot] = acc[spot] + rbufs[g * nb + k][combo + (slice(None), slice(None))]

    def gather_start(buf, order, k, tail, low=0):
        values = list(bit)
        for b in order[:k]:
            values[b] = slice(None)
        ref = buf.at[at(values, low) + tail]
        return remote(ref, ref, order[k])

    barrier = pltpu.get_barrier_semaphore()
    for k in range(1, n):
        pl.semaphore_signal(
            barrier, inc=1, device_id={"wide": lax.rem(me + k, n)}, device_id_type=MESH
        )
    pl.semaphore_wait(barrier, n - 1)

    back = [list(reversed(o)) for o in orders]
    g1[at(bit)] = ta_ref[...] * qp_ref[1:2, :]
    tract_copies = [gather_start(g1, back[g], 0, (slice(None), cols[g])) for g in range(2)]

    tof_row = tof_row_ref[...]
    tof_col = tof_col_ref[...]
    row_hot = (lax.broadcasted_iota(jnp.int32, (groups, blocks), 0) == tof_row // LANES).astype(BF16)
    col_hot = (lax.broadcasted_iota(jnp.int32, (blocks, LANES), 1) == tof_col % LANES).astype(BF16)
    misc[me, :groups, :] = product(row_hot, col_hot)
    lane = lax.broadcasted_iota(jnp.int32, (8, LANES), 1)
    mine = lane // rows == me % (LANES // rows)
    misc[me, groups:, :] = jnp.where(mine, tc_ref[...], 0.0)
    misc_copies = []
    for k in range(1, n):
        copy = pltpu.make_async_remote_copy(
            src_ref=misc.at[me],
            dst_ref=misc.at[me],
            send_sem=misc_send.at[k],
            recv_sem=misc_recv.at[k],
            device_id={"wide": lax.rem(me + k, n)},
            device_id_type=MESH,
        )
        copy.start()
        misc_copies.append(copy)

    xh, xl = halves(ba_ref[...] * qp_ref[0:1, :])
    step = min(4, n)
    for c in range(n // step):
        label = lax.broadcasted_iota(jnp.int32, (step * rows, blocks), 0) + c * step * rows
        hot = (label == tof_row).astype(BF16)
        part = product(hot, xh) + product(hot, xl)
        for s in range(step):
            w = c * step + s
            spot = tuple((w >> b) & 1 for b in range(nb - 1, -1, -1))
            acc[spot] = part[s * rows : (s + 1) * rows]

    sums = [scatter_start(g, 0) for g in range(2)]

    def cover_rows(i, carry):
        start = pl.multiple_of(i * 16, 16)
        label = lax.broadcasted_iota(jnp.int32, (16, cells), 0) + start
        total = jnp.zeros((16, cells), F32)
        for m in range(mt_ref.shape[0]):
            total = total + jnp.where(label == mt_ref[m : m + 1, :], 1.0, 0.0)
        cover_ref[pl.ds(start, 16), :] = total.astype(BF16)
        return carry

    lax.fori_loop(0, queries // 16, cover_rows, 0)
    weights = jnp.concatenate([qp_ref[...], qp_ref[...]], axis=0)
    w0, rest = halves(weights)
    w1, w2 = halves(weights - w0.astype(F32))
    cover = cover_ref[...]
    coverage = product(w0, cover) + product(w1, cover) + product(w2, cover)
    var_ref[...] = 1.0 / coverage

    for k in range(nb):
        for g in range(2):
            sums[g].wait_recv()
            scatter_add(g, k)
            if k + 1 < nb:
                sums[g] = scatter_start(g, k + 1)
        for g in range(2):
            tract_copies[g].wait_recv()
            if k + 1 < nb:
                tract_copies[g] = gather_start(g1, back[g], k + 1, (slice(None), cols[g]))
    gs[at(bit)] = acc[at(bit)]
    sums = [gather_start(gs, back[g], 0, (slice(None), cols[g])) for g in range(2)]

    for copy in misc_copies:
        copy.wait_recv()
    counts = misc[0, :groups, :]
    for d in range(1, n):
        counts = counts + misc[d, :groups, :]
    per = LANES // rows
    county_rows = []
    for j in range(groups):
        row = misc[j * per, groups : groups + 1, :]
        for i in range(1, per):
            row = row + misc[j * per + i, groups : groups + 1, :]
        county_rows.append(row)
    tab_ref[0] = counts
    for j in range(groups):
        tab_ref[1, j : j + 1, :] = county_rows[j]

    def split_into(buf, high_ref, low_ref):
        for w in range(n):
            spot = tuple((w >> b) & 1 for b in range(nb - 1, -1, -1))
            high, low = halves(buf[spot])
            high_ref[w * rows : (w + 1) * rows, :] = high
            low_ref[w * rows : (w + 1) * rows, :] = low

    low_bit = nb - (CHUNKS.bit_length() - 1)
    chunk = me // (1 << low_bit)
    lanes = pl.ds(pl.multiple_of(chunk * LANES, LANES), LANES)
    cov = cover_ref[:, lanes]
    var = var_ref[:, lanes]
    v0, v1, v2, v3 = var[0:1], var[1:2], var[2:3], var[3:4]
    split_into(g1, g1h_ref, g1l_ref)
    tract_part = two_products(g1h_ref[...], g1l_ref[...], cov)
    ch, cl = halves(cs_ref[...])
    upper = two_products(ch, cl, cov)
    county_measured = upper[:counties] * v2
    state_measured = upper[counties : counties + 1] * v3
    n_col = picked(counts, lax.broadcasted_iota(jnp.int32, (n * rows, 1), 0))

    for k in range(nb):
        for g in range(2):
            sums[g].wait_recv()
            if k + 1 < nb:
                sums[g] = gather_start(gs, back[g], k + 1, (slice(None), cols[g]))
    split_into(gs, gsh_ref, gsl_ref)
    sum_part = two_products(gsh_ref[...], gsl_ref[...], cov)
    child_spread = n_col * v0
    scale = 1.0 / (child_spread + v1)
    joined = (n_col * tract_part + sum_part) * (v0 * v1) * scale
    spread = child_spread * v1 * scale
    jh, jl = halves(joined)
    sh, sl = halves(spread)
    county_child = jnp.zeros((counties, LANES), F32)
    county_child_spread = jnp.zeros((counties, LANES), F32)
    for j in range(groups):
        label = lax.broadcasted_iota(jnp.int32, (counties, LANES), 0).astype(F32)
        hot = (label == county_rows[j]).astype(BF16)
        piece = slice(j * LANES, (j + 1) * LANES)
        county_child += product(hot, jh[piece]) + product(hot, jl[piece])
        county_child_spread += product(hot, sh[piece]) + product(hot, sl[piece])
    county_total = county_child_spread + v2
    county_joined = (county_child_spread * county_measured + v2 * county_child) / county_total
    county_spread = county_child_spread * v2 / county_total
    state_sum = jnp.sum(county_joined, axis=0, keepdims=True)
    state_spread = jnp.sum(county_spread, axis=0, keepdims=True)
    state_rate = (state_measured - state_sum) / (state_spread + v3)
    spot = at(bit, low_bit)
    g2[spot + (0,)] = (county_measured - county_child + v2 * state_rate) / county_total
    g2[spot + (1,)] = county_joined + county_spread * state_rate
    short = [[b for b in o if b >= low_bit] for o in back]
    last = [gather_start(g2, short[g], 0, (g,), low_bit) for g in range(2)]
    for k in range(len(short[0])):
        for g in range(2):
            last[g].wait_recv()
            if k + 1 < len(short[0]):
                last[g] = gather_start(g2, short[g], k + 1, (g,), low_bit)
    for c in range(CHUNKS):
        spot = tuple((c >> b) & 1 for b in range(CHUNKS.bit_length() - 2, -1, -1))
        rate_ref[:, c * LANES : (c + 1) * LANES] = g2[spot + (0,)]
        hist_ref[:, c * LANES : (c + 1) * LANES] = g2[spot + (1,)]
    for copy in sends + misc_copies:
        copy.wait_send()


def histogram_kernel(
    ba_ref,
    tof_ref,
    own_ref,
    qp_ref,
    g1h_ref,
    g1l_ref,
    gsh_ref,
    gsl_ref,
    cover_ref,
    var_ref,
    tab_ref,
    rate_ref,
    hist_ref,
    block_ref,
    tract_ref,
    county_ref,
):
    cells = block_ref.shape[1]
    tracts = g1h_ref.shape[0]
    counties = rate_ref.shape[0]
    width = 512

    def gathered(ids):
        count = ids.shape[0]
        hot = (lax.broadcasted_iota(jnp.int32, (count, tracts), 1) == ids).astype(BF16)
        parts = [product(hot, ref[...]).astype(BF16) for ref in (g1h_ref, g1l_ref, gsh_ref, gsl_ref)]
        n_col = picked(tab_ref[0], ids)
        county = picked(tab_ref[1], ids)
        label = lax.broadcasted_iota(jnp.int32, (count, counties), 1).astype(F32)
        return parts, n_col, (label == county).astype(BF16)

    def pieces(start, stop, parts, county_hot):
        cov = cover_ref[:, start:stop]
        rh, rl = halves(rate_ref[:, start:stop])
        above = product(county_hot, rh) + product(county_hot, rl)
        return (
            cov,
            var_ref[0:1, start:stop],
            var_ref[1:2, start:stop],
            two_products(parts[0], parts[1], cov),
            two_products(parts[2], parts[3], cov),
            above,
        )

    parts, n_col, county_hot = gathered(tof_ref[...])
    xh, xl = halves(ba_ref[...] * qp_ref[0:1, :])
    for start in range(0, cells, width):
        stop = min(cells, start + width)
        cov, v0, v1, tract_part, sum_part, above = pieces(start, stop, parts, county_hot)
        rate = (v1 * (tract_part + above) - v0 * sum_part) / (n_col * v0 + v1)
        block_ref[:, start:stop] = v0 * (two_products(xh, xl, cov) + rate)

    @pl.when(pl.program_id(0) == 0)
    def _():
        parts, n_col, county_hot = gathered(own_ref[...])
        for start in range(0, cells, width):
            stop = min(cells, start + width)
            cov, v0, v1, tract_part, sum_part, above = pieces(start, stop, parts, county_hot)
            top = n_col * tract_part + sum_part + n_col * above
            tract_ref[:, start:stop] = v0 * v1 * top / (n_col * v0 + v1)
        county_ref[...] = hist_ref[:, :cells]


def local(
    block_answers,
    block_owner,
    block_place,
    tract_answers,
    tract_county,
    county_answers,
    state_answers,
    query_members,
    query_precision,
):
    n = lax.axis_size("wide")
    nb = n.bit_length() - 1
    blocks, queries = block_answers.shape
    rows = tract_answers.shape[0]
    tracts = rows * n
    cells = query_members.shape[0]
    counties = county_answers.shape[0]
    padded = CHUNKS * LANES
    groups = tracts // LANES
    half = queries // 2
    tof_col = block_owner * rows + block_place[:, None]
    tof_row = block_owner[:, 0][None, :] * rows + block_place[None, :]
    tc = jnp.tile(tract_county.astype(F32), LANES // rows)[None, :]
    cs = jnp.concatenate(
        [
            county_answers * query_precision[2:3],
            state_answers * query_precision[3:4],
            jnp.zeros((-(counties + 1) % 16, queries), F32),
        ]
    )
    mt = jnp.pad(query_members.T, ((0, 0), (0, padded - cells)))
    vmem = pl.BlockSpec(memory_space=pltpu.VMEM)
    binary = (2,) * nb
    copies = 8 * nb
    shape = jax.ShapeDtypeStruct
    rbufs = [
        pltpu.VMEM((2,) * (nb - k - 1) + (rows, half), F32) for _ in range(2) for k in range(nb)
    ]
    outs = pl.pallas_call(
        functools.partial(tree_kernel, n),
        out_shape=[shape((tracts, queries), BF16)] * 4
        + [
            shape((queries, padded), BF16),
            shape((8, padded), F32),
            shape((2, groups, LANES), F32),
            shape((counties, padded), F32),
            shape((counties, padded), F32),
        ],
        in_specs=[vmem] * 8,
        out_specs=[vmem] * 9,
        scratch_shapes=[
            pltpu.VMEM(binary + (rows, queries), F32),
            pltpu.VMEM(binary + (rows, queries), F32),
            pltpu.VMEM(binary + (rows, queries), F32),
            pltpu.VMEM((2,) * (CHUNKS.bit_length() - 1) + (2, counties, LANES), F32),
            pltpu.VMEM((n, groups + 8, LANES), F32),
            pltpu.SemaphoreType.DMA((n,)),
            pltpu.SemaphoreType.DMA((n,)),
            pltpu.SemaphoreType.DMA((copies,)),
            pltpu.SemaphoreType.DMA((copies,)),
        ]
        + rbufs,
        compiler_params=pltpu.CompilerParams(
            collective_id=0, has_side_effects=True, vmem_limit_bytes=56 * 1024 * 1024
        ),
        name="tree",
    )(block_answers, tof_row, tof_col, tract_answers, tc, cs, mt, query_precision)

    own = (lax.axis_index("wide") * rows + jnp.arange(rows, dtype=jnp.int32))[:, None]
    tile = 256
    whole = lambda a: pl.BlockSpec(a.shape, lambda i: (0,) * a.ndim)
    return pl.pallas_call(
        histogram_kernel,
        grid=(blocks // tile,),
        out_shape=[
            shape((blocks, cells), F32),
            shape((rows, cells), F32),
            shape((counties, cells), F32),
        ],
        in_specs=[
            pl.BlockSpec((tile, queries), lambda i: (i, 0)),
            pl.BlockSpec((tile, 1), lambda i: (i, 0)),
            whole(own),
            whole(query_precision),
        ]
        + [whole(a) for a in outs],
        out_specs=[
            pl.BlockSpec((tile, cells), lambda i: (i, 0)),
            pl.BlockSpec((rows, cells), lambda i: (0, 0)),
            pl.BlockSpec((counties, cells), lambda i: (0, 0)),
        ],
        compiler_params=pltpu.CompilerParams(vmem_limit_bytes=56 * 1024 * 1024),
        name="histograms",
    )(block_answers, tof_col, own, query_precision, *outs)


def solution(mesh):
    in_specs = (
        P(("state", "wide"), None),
        P(("state", "wide"), None),
        P(("state", "wide")),
        P(("state", "wide"), None),
        P(("state", "wide")),
        P("state", None),
        P("state", None),
        P(),
        P(),
    )
    out_specs = (P(("state", "wide"), None), P(("state", "wide"), None), P("state", None))
    return jax.shard_map(local, mesh=mesh, in_specs=in_specs, out_specs=out_specs, check_vma=False)
```

```python
import functools
import itertools

import jax
import jax.numpy as jnp
from jax import lax
from jax.experimental import pallas as pl
from jax.experimental.pallas import tpu as pltpu
from jax.sharding import PartitionSpec as P

LANES = 128
CHUNKS = 16
MESH = pl.DeviceIdType.MESH
F32 = jnp.float32
BF16 = jnp.bfloat16


def halves(x):
    high = x.astype(BF16)
    return high, (x - high.astype(F32)).astype(BF16)


def product(left, right):
    return jnp.dot(left, right, preferred_element_type=F32)


def two_products(high, low, right):
    return product(high, right) + product(low, right)


def picked(table, row_of):
    groups = table.shape[0]
    count = row_of.shape[0]
    wide = jnp.zeros((count, LANES), F32)
    for g in range(groups):
        wide = jnp.where(row_of // LANES == g, table[g : g + 1, :], wide)
    lane = lax.broadcasted_iota(jnp.int32, (count, LANES), 1)
    return jnp.sum(jnp.where(lane == row_of % LANES, wide, 0.0), axis=1, keepdims=True)


def nt_product(left, right):
    return lax.dot_general(left, right, (((1,), (1,)), ((), ())), preferred_element_type=F32)


def tree_kernel(
    n,
    ba_ref,
    owner_ref,
    place_ref,
    ta_ref,
    tc_ref,
    ca_ref,
    sa_ref,
    mt_ref,
    qp_ref,
    base_ref,
    cov_ref,
    covt_ref,
    nk_ref,
    own_ref,
    tbase_ref,
    rate_ref,
    hist_ref,
    acc,
    g1,
    gs,
    g2,
    misc,
    mpad,
    cover_ref,
    covert_ref,
    tofc,
    high_ref,
    low_ref,
    misc_send,
    misc_recv,
    send_sems,
    recv_sems,
    *rbufs,
):
    nb = n.bit_length() - 1
    me = lax.axis_index("wide")
    rows, queries = ta_ref.shape
    blocks = ba_ref.shape[0]
    cells = cover_ref.shape[1]
    groups = n * rows // LANES
    counties = rate_ref.shape[0]
    tile = 256
    tall = 512
    half = queries // 2
    bit = [(me // (1 << b)) % 2 for b in range(nb)]
    orders = [list(range(nb)), [0] + list(range(2, nb)) + [1]]
    cols = [pl.ds(0, half), pl.ds(half, half)]
    used = [0]
    sends = []

    def partner(b):
        return me + (1 - 2 * bit[b]) * (1 << b)

    def remote(src, dst, b):
        k = used[0]
        used[0] += 1
        copy = pltpu.make_async_remote_copy(
            src_ref=src,
            dst_ref=dst,
            send_sem=send_sems.at[k],
            recv_sem=recv_sems.at[k],
            device_id={"wide": partner(b)},
            device_id_type=MESH,
        )
        copy.start()
        sends.append(copy)
        return copy

    def at(values, low=0):
        return tuple(values[b] for b in range(nb - 1, low - 1, -1))

    def scatter_start(g, k):
        order = orders[g]
        values = [slice(None)] * nb
        for b in order[:k]:
            values[b] = bit[b]
        values[order[k]] = 1 - bit[order[k]]
        src = acc.at[at(values) + (slice(None), cols[g])]
        return remote(src, rbufs[g * nb + k], order[k])

    def scatter_add(g, k):
        order = orders[g]
        rest = sorted(order[k + 1 :], reverse=True)
        for combo in itertools.product((0, 1), repeat=len(rest)):
            values = list(bit)
            for b, v in zip(rest, combo):
                values[b] = v
            spot = at(values) + (slice(None), cols[g])
            acc[spot] = acc[spot] + rbufs[g * nb + k][combo + (slice(None), slice(None))]

    def gather_start(buf, order, k, tail, low=0):
        values = list(bit)
        for b in order[:k]:
            values[b] = slice(None)
        ref = buf.at[at(values, low) + tail]
        return remote(ref, ref, order[k])

    barrier = pltpu.get_barrier_semaphore()
    for k in range(1, n):
        pl.semaphore_signal(
            barrier, inc=1, device_id={"wide": lax.rem(me + k, n)}, device_id_type=MESH
        )
    pl.semaphore_wait(barrier, n - 1)

    back = [list(reversed(o)) for o in orders]
    g1[at(bit)] = ta_ref[...] * qp_ref[1:2, :]
    tract_copies = [gather_start(g1, back[g], 0, (slice(None), cols[g])) for g in range(2)]

    tof_row = owner_ref[...] * rows + place_ref[...]
    tofc[...] = jnp.broadcast_to(tof_row.astype(F32), (LANES, blocks)).T.astype(jnp.int32)
    tof_col = tofc[:, 0:1]
    row_hot = (lax.broadcasted_iota(jnp.int32, (groups, blocks), 0) == tof_row // LANES).astype(BF16)
    col_hot = (lax.broadcasted_iota(jnp.int32, (blocks, LANES), 1) == tof_col % LANES).astype(BF16)
    misc[me, :groups, :] = product(row_hot, col_hot)
    lane = lax.broadcasted_iota(jnp.int32, (8, LANES), 1)
    mine = lane // rows == me % (LANES // rows)
    misc[me, groups:, :] = jnp.where(mine, jnp.concatenate([tc_ref[...].astype(F32)] * (LANES // rows), axis=1), 0.0)
    misc_copies = []
    for k in range(1, n):
        copy = pltpu.make_async_remote_copy(
            src_ref=misc.at[me],
            dst_ref=misc.at[me],
            send_sem=misc_send.at[k],
            recv_sem=misc_recv.at[k],
            device_id={"wide": lax.rem(me + k, n)},
            device_id_type=MESH,
        )
        copy.start()
        misc_copies.append(copy)

    xh, xl = halves(ba_ref[...] * qp_ref[0:1, :])
    step = min(4, n)
    for c in range(n // step):
        label = lax.broadcasted_iota(jnp.int32, (step * rows, blocks), 0) + c * step * rows
        hot = (label == tof_row).astype(BF16)
        part = product(hot, xh) + product(hot, xl)
        for s in range(step):
            w = c * step + s
            spot = tuple((w >> b) & 1 for b in range(nb - 1, -1, -1))
            acc[spot] = part[s * rows : (s + 1) * rows]

    sums = [scatter_start(g, 0) for g in range(2)]

    mpad[...] = jnp.zeros_like(mpad)
    mpad[:, : mt_ref.shape[1]] = mt_ref[...]

    def cover_lanes(i, carry):
        spot = pl.ds(pl.multiple_of(i * LANES, LANES), LANES)
        label = lax.broadcasted_iota(jnp.int32, (queries, LANES), 0)
        total = jnp.zeros((queries, LANES), F32)
        for m in range(mpad.shape[0]):
            total = total + jnp.where(label == mpad[m : m + 1, spot], 1.0, 0.0)
        cover_ref[:, spot] = total.astype(BF16)
        covert_ref[spot, :] = total.T.astype(BF16)
        return carry

    lax.fori_loop(0, cells // LANES, cover_lanes, 0)
    weights = jnp.concatenate([qp_ref[...], qp_ref[...]], axis=0)
    w0, _ = halves(weights)
    w1, w2 = halves(weights - w0.astype(F32))
    cover = cover_ref[...]
    coverage = product(w0, cover) + product(w1, cover) + product(w2, cover)
    cov_ref[...] = coverage
    blank = jnp.zeros((LANES - 8, LANES), F32)
    for c in range(cells // LANES):
        piece = slice(c * LANES, (c + 1) * LANES)
        covt_ref[piece, :] = jnp.concatenate([coverage[:, piece], blank], axis=0).T

    def blocks_part(j):
        spot = slice(j * tile, (j + 1) * tile)
        xh, xl = halves(ba_ref[spot, :] * qp_ref[0:1, :])

        def body(i, carry):
            down = pl.ds(pl.multiple_of(i * tall, tall), tall)
            left = covert_ref[down, :]
            total = nt_product(left, xh) + nt_product(left, xl)
            base_ref[down, spot] = total * (1.0 / covt_ref[down, 0:1])
            return carry

        lax.fori_loop(0, cells // tall, body, 0)

    def tracts_part(j, of_sums):
        spot = slice(j * tile, (j + 1) * tile)
        label = lax.broadcasted_iota(jnp.int32, (tile, n * rows), 1)
        hot = (label == tofc[spot, 0:1]).astype(BF16)
        ph = product(hot, high_ref[...]).astype(BF16)
        pl_ = product(hot, low_ref[...]).astype(BF16)
        n_row = nk_ref[0:1, spot]

        def body(i, carry):
            down = pl.ds(pl.multiple_of(i * tall, tall), tall)
            left = covert_ref[down, :]
            total = nt_product(left, ph) + nt_product(left, pl_)
            c0, c1 = covt_ref[down, 0:1], covt_ref[down, 1:2]
            if of_sums:
                total = total * (-c1 / c0)
            base_ref[down, spot] = base_ref[down, spot] + total / (n_row * c1 + c0)
            return carry

        lax.fori_loop(0, cells // tall, body, 0)

    parts = blocks // tile
    for k in range(nb):
        if k:
            for j in range(parts):
                if j % (nb - 1) == k - 1:
                    blocks_part(j)
        for g in range(2):
            sums[g].wait_recv()
            scatter_add(g, k)
            if k + 1 < nb:
                sums[g] = scatter_start(g, k + 1)
        for g in range(2):
            tract_copies[g].wait_recv()
            if k + 1 < nb:
                tract_copies[g] = gather_start(g1, back[g], k + 1, (slice(None), cols[g]))
    gs[at(bit)] = acc[at(bit)]
    sums = [gather_start(gs, back[g], 0, (slice(None), cols[g])) for g in range(2)]

    for copy in misc_copies:
        copy.wait_recv()
    counts = misc[0, :groups, :]
    for d in range(1, n):
        counts = counts + misc[d, :groups, :]
    per = LANES // rows
    county_rows = []
    for j in range(groups):
        row = misc[j * per, groups : groups + 1, :]
        for i in range(1, per):
            row = row + misc[j * per + i, groups : groups + 1, :]
        county_rows.append(row)
    county_table = jnp.concatenate(county_rows, axis=0)
    n_col = picked(counts, lax.broadcasted_iota(jnp.int32, (n * rows, 1), 0))
    nk_ref[0:1, :] = jnp.broadcast_to(picked(counts, tofc[:, 0:1]), (blocks, LANES)).T[0:1]
    nk_ref[1:2, :] = jnp.broadcast_to(picked(county_table, tofc[:, 0:1]), (blocks, LANES)).T[0:1]
    mine_id = lax.broadcasted_iota(jnp.int32, (rows, 1), 0) + me * rows
    n_own = picked(counts, mine_id)
    own_ref[:, 0:1] = n_own
    own_ref[:, 1:2] = picked(county_table, mine_id)

    def spot_of(w):
        return tuple((w >> b) & 1 for b in range(nb - 1, -1, -1))

    def split_into(value_of):
        for w in range(n):
            high, low = halves(value_of(w))
            high_ref[w * rows : (w + 1) * rows, :] = high
            low_ref[w * rows : (w + 1) * rows, :] = low

    def stacked(x, right):
        high, low = halves(x)
        both = product(jnp.concatenate([high, low], axis=0), right)
        return both[: x.shape[0]] + both[x.shape[0] :]

    low_bit = nb - (CHUNKS.bit_length() - 1)
    chunk = me // (1 << low_bit)
    lanes = pl.ds(pl.multiple_of(chunk * LANES, LANES), LANES)
    cov = cover_ref[:, lanes]
    c0, c1, c2, c3 = [cov_ref[l : l + 1, lanes] for l in range(4)]
    v2, v3 = 1.0 / c2, 1.0 / c3
    county_measured = stacked(ca_ref[...] * qp_ref[2:3, :], cov) * v2
    state_row = jnp.broadcast_to(sa_ref[...] * qp_ref[3:4, :], (16, queries))
    state_measured = stacked(state_row, cov)[0:1] * v3
    split_into(lambda w: g1[spot_of(w)])

    for k in range(nb):
        for j in range(parts):
            if j % nb == k:
                tracts_part(j, False)
        if k == 0:
            own_sum = n_own * (ta_ref[...] * qp_ref[1:2, :]) + acc[at(bit)]
            tbase_ref[...] = stacked(own_sum, cover_ref[...])
        for g in range(2):
            sums[g].wait_recv()
            if k + 1 < nb:
                sums[g] = gather_start(gs, back[g], k + 1, (slice(None), cols[g]))
    split_into(lambda w: n_col[w * rows : (w + 1) * rows] * g1[spot_of(w)] + gs[spot_of(w)])
    total = two_products(high_ref[...], low_ref[...], cov)
    factor = 1.0 / (n_col * c1 + c0)
    joined = total * factor
    spread = n_col * factor
    jh, jl = halves(joined)
    sh, sl = halves(spread)
    both = jnp.concatenate([jh, jl, sh, sl], axis=1)
    sums4 = jnp.zeros((counties, 4 * LANES), F32)
    for j in range(groups):
        label = lax.broadcasted_iota(jnp.int32, (counties, LANES), 0).astype(F32)
        hot = (label == county_rows[j]).astype(BF16)
        sums4 += product(hot, both[j * LANES : (j + 1) * LANES])
    county_child = sums4[:, :LANES] + sums4[:, LANES : 2 * LANES]
    county_child_spread = sums4[:, 2 * LANES : 3 * LANES] + sums4[:, 3 * LANES :]
    county_total = county_child_spread + v2
    county_joined = (county_child_spread * county_measured + v2 * county_child) / county_total
    county_spread = county_child_spread * v2 / county_total
    state_sum = jnp.sum(county_joined, axis=0, keepdims=True)
    state_spread = jnp.sum(county_spread, axis=0, keepdims=True)
    state_rate = (state_measured - state_sum) / (state_spread + v3)
    spot = at(bit, low_bit)
    g2[spot + (0,)] = (county_measured - county_child + v2 * state_rate) / county_total
    g2[spot + (1,)] = county_joined + county_spread * state_rate
    short = [[b for b in o if b >= low_bit] for o in back]
    last = [gather_start(g2, short[g], 0, (g,), low_bit) for g in range(2)]
    split_into(lambda w: gs[spot_of(w)])
    for k in range(len(short[0])):
        for j in range(parts):
            if j % len(short[0]) == k:
                tracts_part(j, True)
        for g in range(2):
            last[g].wait_recv()
            if k + 1 < len(short[0]):
                last[g] = gather_start(g2, short[g], k + 1, (g,), low_bit)
    for c in range(CHUNKS):
        spot = tuple((c >> b) & 1 for b in range(CHUNKS.bit_length() - 2, -1, -1))
        rate_ref[:, c * LANES : (c + 1) * LANES] = g2[spot + (0,)]
        hist_ref[:, c * LANES : (c + 1) * LANES] = g2[spot + (1,)]
    for copy in sends + misc_copies:
        copy.wait_send()


def histogram_kernel(
    base_ref, cov_ref, covt_ref, nk_ref, own_ref, tbase_ref, rate_ref, hist_ref,
    block_ref, tract_ref, county_ref,
):
    counties, width = rate_ref.shape
    blocks = nk_ref.shape[1]
    rows = own_ref.shape[0]
    rate = jnp.concatenate([rate_ref[...], jnp.zeros((LANES - counties, width), F32)], axis=0)
    rh, rl = halves(rate.T)
    label = lax.broadcasted_iota(jnp.int32, (LANES, blocks), 0).astype(F32)
    hot = (label == nk_ref[1:2, :]).astype(BF16)
    above = two_products(rh, rl, hot)
    c0, c1 = covt_ref[:, 0:1], covt_ref[:, 1:2]
    block_ref[...] = base_ref[...] + above / (nk_ref[0:1, :] * c1 + c0)

    label = lax.broadcasted_iota(jnp.int32, (rows, LANES), 1).astype(F32)
    hot = (label == own_ref[:, 1:2]).astype(BF16)
    rh, rl = halves(rate)
    n_own = own_ref[:, 0:1]
    above = product(hot, rh) + product(hot, rl)
    tract_ref[...] = (tbase_ref[...] + n_own * above) / (n_own * cov_ref[1:2, :] + cov_ref[0:1, :])
    county_ref[...] = hist_ref[...]


def local(
    block_answers,
    block_owner,
    block_place,
    tract_answers,
    tract_county,
    county_answers,
    state_answers,
    query_members,
    query_precision,
):
    n = lax.axis_size("wide")
    nb = n.bit_length() - 1
    blocks, queries = block_answers.shape
    rows = tract_answers.shape[0]
    tracts = rows * n
    cells = query_members.shape[0]
    counties = county_answers.shape[0]
    padded = CHUNKS * LANES
    groups = tracts // LANES
    half = queries // 2
    vmem = pl.BlockSpec(memory_space=pltpu.VMEM)
    binary = (2,) * nb
    copies = 8 * nb
    shape = jax.ShapeDtypeStruct
    rbufs = [
        pltpu.VMEM((2,) * (nb - k - 1) + (rows, half), F32) for _ in range(2) for k in range(nb)
    ]
    outs = pl.pallas_call(
        functools.partial(tree_kernel, n),
        out_shape=[
            shape((padded, blocks), F32),
            shape((8, padded), F32),
            shape((padded, LANES), F32),
            shape((8, blocks), F32),
            shape((rows, LANES), F32),
            shape((rows, padded), F32),
            shape((counties, padded), F32),
            shape((counties, padded), F32),
        ],
        in_specs=[vmem] * 9,
        out_specs=[vmem] * 8,
        scratch_shapes=[
            pltpu.VMEM(binary + (rows, queries), F32),
            pltpu.VMEM(binary + (rows, queries), F32),
            pltpu.VMEM(binary + (rows, queries), F32),
            pltpu.VMEM((2,) * (CHUNKS.bit_length() - 1) + (2, counties, LANES), F32),
            pltpu.VMEM((n, groups + 8, LANES), F32),
            pltpu.VMEM((query_members.shape[1], padded), jnp.int32),
            pltpu.VMEM((queries, padded), BF16),
            pltpu.VMEM((padded, queries), BF16),
            pltpu.VMEM((blocks, LANES), jnp.int32),
            pltpu.VMEM((tracts, queries), BF16),
            pltpu.VMEM((tracts, queries), BF16),
            pltpu.SemaphoreType.DMA((n,)),
            pltpu.SemaphoreType.DMA((n,)),
            pltpu.SemaphoreType.DMA((copies,)),
            pltpu.SemaphoreType.DMA((copies,)),
        ]
        + rbufs,
        compiler_params=pltpu.CompilerParams(
            collective_id=0, has_side_effects=True, vmem_limit_bytes=56 * 1024 * 1024
        ),
        name="tree",
    )(
        block_answers,
        block_owner.T,
        block_place[None, :],
        tract_answers,
        tract_county[None, :],
        county_answers,
        state_answers,
        query_members.T,
        query_precision,
    )

    tile = 256
    down = lambda a: pl.BlockSpec((tile, a.shape[1]), lambda i: (i, 0))
    across = lambda a: pl.BlockSpec((a.shape[0], tile), lambda i: (0, i))
    whole = lambda a: pl.BlockSpec(a.shape, lambda i: (0, 0))
    kinds = [down, across, down, whole, whole, across, across, across]
    block_histogram, tract_histogram, county_histogram = pl.pallas_call(
        histogram_kernel,
        grid=(padded // tile,),
        out_shape=[
            shape((cells, blocks), F32),
            shape((rows, cells), F32),
            shape((counties, cells), F32),
        ],
        in_specs=[kind(a) for kind, a in zip(kinds, outs)],
        out_specs=[
            pl.BlockSpec((tile, blocks), lambda i: (i, 0)),
            pl.BlockSpec((rows, tile), lambda i: (0, i)),
            pl.BlockSpec((counties, tile), lambda i: (0, i)),
        ],
        compiler_params=pltpu.CompilerParams(vmem_limit_bytes=56 * 1024 * 1024),
        name="histograms",
    )(*outs)
    return block_histogram.T, tract_histogram, county_histogram


def solution(mesh):
    in_specs = (
        P(("state", "wide"), None),
        P(("state", "wide"), None),
        P(("state", "wide")),
        P(("state", "wide"), None),
        P(("state", "wide")),
        P("state", None),
        P("state", None),
        P(),
        P(),
    )
    out_specs = (P(("state", "wide"), None), P(("state", "wide"), None), P("state", None))
    return jax.shard_map(local, mesh=mesh, in_specs=in_specs, out_specs=out_specs, check_vma=False)
```

```python
import functools
import itertools

import jax
import jax.numpy as jnp
from jax import lax
from jax.experimental import pallas as pl
from jax.experimental.pallas import tpu as pltpu
from jax.sharding import PartitionSpec as P

LANES = 128
CHUNKS = 16
MESH = pl.DeviceIdType.MESH
F32 = jnp.float32
BF16 = jnp.bfloat16


def halves(x):
    high = x.astype(BF16)
    return high, (x - high.astype(F32)).astype(BF16)


def product(left, right):
    return jnp.dot(left, right, preferred_element_type=F32)


def two_products(high, low, right):
    return product(high, right) + product(low, right)


def picked(table, row_of):
    groups = table.shape[0]
    count = row_of.shape[0]
    wide = jnp.zeros((count, LANES), F32)
    for g in range(groups):
        wide = jnp.where(row_of // LANES == g, table[g : g + 1, :], wide)
    lane = lax.broadcasted_iota(jnp.int32, (count, LANES), 1)
    return jnp.sum(jnp.where(lane == row_of % LANES, wide, 0.0), axis=1, keepdims=True)


def nt_product(left, right):
    return lax.dot_general(left, right, (((1,), (1,)), ((), ())), preferred_element_type=F32)


def tree_kernel(
    n,
    ba_ref,
    owner_ref,
    place_ref,
    ta_ref,
    tc_ref,
    ca_ref,
    sa_ref,
    mt_ref,
    qp_ref,
    base_ref,
    cov_ref,
    covt_ref,
    nk_ref,
    own_ref,
    tbase_ref,
    rate_ref,
    hist_ref,
    acc,
    g1,
    gs,
    g2,
    misc,
    mpad,
    cover_ref,
    covert_ref,
    tofc,
    high_ref,
    low_ref,
    misc_send,
    misc_recv,
    send_sems,
    recv_sems,
    *rbufs,
):
    nb = n.bit_length() - 1
    me = lax.axis_index("wide")
    rows, queries = ta_ref.shape
    blocks = ba_ref.shape[0]
    cells = cover_ref.shape[1]
    groups = n * rows // LANES
    counties = rate_ref.shape[0]
    tile = 256
    tall = 512
    half = queries // 2
    bit = [(me // (1 << b)) % 2 for b in range(nb)]
    orders = [list(range(nb)), [0] + list(range(2, nb)) + [1]]
    cols = [pl.ds(0, half), pl.ds(half, half)]
    used = [0]
    sends = []

    def partner(b):
        return me + (1 - 2 * bit[b]) * (1 << b)

    def remote(src, dst, b):
        k = used[0]
        used[0] += 1
        copy = pltpu.make_async_remote_copy(
            src_ref=src,
            dst_ref=dst,
            send_sem=send_sems.at[k],
            recv_sem=recv_sems.at[k],
            device_id={"wide": partner(b)},
            device_id_type=MESH,
        )
        copy.start()
        sends.append(copy)
        return copy

    def at(values, low=0):
        return tuple(values[b] for b in range(nb - 1, low - 1, -1))

    def scatter_start(g, k):
        order = orders[g]
        values = [slice(None)] * nb
        for b in order[:k]:
            values[b] = bit[b]
        values[order[k]] = 1 - bit[order[k]]
        src = acc.at[at(values) + (slice(None), cols[g])]
        return remote(src, rbufs[g * nb + k], order[k])

    def scatter_add(g, k):
        order = orders[g]
        rest = sorted(order[k + 1 :], reverse=True)
        for combo in itertools.product((0, 1), repeat=len(rest)):
            values = list(bit)
            for b, v in zip(rest, combo):
                values[b] = v
            spot = at(values) + (slice(None), cols[g])
            acc[spot] = acc[spot] + rbufs[g * nb + k][combo + (slice(None), slice(None))]

    def gather_start(buf, order, k, tail, low=0):
        values = list(bit)
        for b in order[:k]:
            values[b] = slice(None)
        ref = buf.at[at(values, low) + tail]
        return remote(ref, ref, order[k])

    barrier = pltpu.get_barrier_semaphore()
    for k in range(1, n):
        pl.semaphore_signal(
            barrier, inc=1, device_id={"wide": lax.rem(me + k, n)}, device_id_type=MESH
        )
    pl.semaphore_wait(barrier, n - 1)

    back = [list(reversed(o)) for o in orders]
    g1[at(bit)] = ta_ref[...] * qp_ref[1:2, :]
    tract_copies = [gather_start(g1, back[g], 0, (slice(None), cols[g])) for g in range(2)]

    tof_row = owner_ref[...] * rows + place_ref[...]
    tofc[...] = jnp.broadcast_to(tof_row.astype(F32), (LANES, blocks)).T.astype(jnp.int32)
    tof_col = tofc[:, 0:1]
    row_hot = (lax.broadcasted_iota(jnp.int32, (groups, blocks), 0) == tof_row // LANES).astype(BF16)
    col_hot = (lax.broadcasted_iota(jnp.int32, (blocks, LANES), 1) == tof_col % LANES).astype(BF16)
    misc[me, :groups, :] = product(row_hot, col_hot)
    lane = lax.broadcasted_iota(jnp.int32, (8, LANES), 1)
    mine = lane // rows == me % (LANES // rows)
    misc[me, groups:, :] = jnp.where(mine, jnp.concatenate([tc_ref[...].astype(F32)] * (LANES // rows), axis=1), 0.0)
    misc_copies = []
    for k in range(1, n):
        copy = pltpu.make_async_remote_copy(
            src_ref=misc.at[me],
            dst_ref=misc.at[me],
            send_sem=misc_send.at[k],
            recv_sem=misc_recv.at[k],
            device_id={"wide": lax.rem(me + k, n)},
            device_id_type=MESH,
        )
        copy.start()
        misc_copies.append(copy)

    xh, xl = halves(ba_ref[...] * qp_ref[0:1, :])
    step = min(4, n)
    for c in range(n // step):
        label = lax.broadcasted_iota(jnp.int32, (step * rows, blocks), 0) + c * step * rows
        hot = (label == tof_row).astype(BF16)
        part = product(hot, xh) + product(hot, xl)
        for s in range(step):
            w = c * step + s
            spot = tuple((w >> b) & 1 for b in range(nb - 1, -1, -1))
            acc[spot] = part[s * rows : (s + 1) * rows]

    def tract_step(k):
        for g in range(2):
            tract_copies[g].wait_recv()
            if k + 1 < nb:
                tract_copies[g] = gather_start(g1, back[g], k + 1, (slice(None), cols[g]))

    tract_step(0)
    sums = [scatter_start(g, 0) for g in range(2)]

    mpad[...] = jnp.zeros_like(mpad)
    mpad[:, : mt_ref.shape[1]] = mt_ref[...]

    def cover_lanes(i, carry):
        spot = pl.ds(pl.multiple_of(i * LANES, LANES), LANES)
        label = lax.broadcasted_iota(jnp.int32, (queries, LANES), 0)
        total = jnp.zeros((queries, LANES), F32)
        for m in range(mpad.shape[0]):
            total = total + jnp.where(label == mpad[m : m + 1, spot], 1.0, 0.0)
        cover_ref[:, spot] = total.astype(BF16)
        covert_ref[spot, :] = total.T.astype(BF16)
        return carry

    lax.fori_loop(0, cells // LANES, cover_lanes, 0)
    weights = jnp.concatenate([qp_ref[...], qp_ref[...]], axis=0)
    w0, _ = halves(weights)
    w1, w2 = halves(weights - w0.astype(F32))
    cover = cover_ref[...]
    coverage = product(w0, cover) + product(w1, cover) + product(w2, cover)
    cov_ref[...] = coverage
    blank = jnp.zeros((LANES - 8, LANES), F32)
    for c in range(cells // LANES):
        piece = slice(c * LANES, (c + 1) * LANES)
        covt_ref[piece, :] = jnp.concatenate([coverage[:, piece], blank], axis=0).T

    def tracts_part(j, of_sums):
        spot = slice(j * tile, (j + 1) * tile)
        label = lax.broadcasted_iota(jnp.int32, (tile, n * rows), 1)
        hot = (label == tofc[spot, 0:1]).astype(BF16)
        ph = product(hot, high_ref[...]).astype(BF16)
        pl_ = product(hot, low_ref[...]).astype(BF16)
        n_row = nk_ref[0:1, spot]
        if not of_sums:
            near = ph.astype(F32) + pl_.astype(F32) + ba_ref[spot, :] * qp_ref[0:1, :]
            ph, pl_ = halves(near)

        def body(i, carry):
            down = pl.ds(pl.multiple_of(i * tall, tall), tall)
            left = covert_ref[down, :]
            total = nt_product(left, ph) + nt_product(left, pl_)
            c0, c1 = covt_ref[down, 0:1], covt_ref[down, 1:2]
            if of_sums:
                scaled = total * (c1 / c0) / (n_row * c1 + c0)
                base_ref[down, spot] = base_ref[down, spot] - scaled
            else:
                base_ref[down, spot] = total * (1.0 / c0)
            return carry

        lax.fori_loop(0, cells // tall, body, 0)

    parts = blocks // tile
    for k in range(nb):
        for g in range(2):
            sums[g].wait_recv()
            scatter_add(g, k)
            if k + 1 < nb:
                sums[g] = scatter_start(g, k + 1)
        if k != 1 and k < nb - 1:
            tract_step(1 if k == 0 else k)

    for copy in misc_copies:
        copy.wait_recv()
    counts = misc[0, :groups, :]
    for d in range(1, n):
        counts = counts + misc[d, :groups, :]
    mine_id = lax.broadcasted_iota(jnp.int32, (rows, 1), 0) + me * rows
    n_own = picked(counts, mine_id)
    own_sum = n_own * (ta_ref[...] * qp_ref[1:2, :]) + acc[at(bit)]
    gs[at(bit)] = own_sum
    sums = [gather_start(gs, back[g], 0, (slice(None), cols[g])) for g in range(2)]
    tract_step(nb - 1)

    per = LANES // rows
    county_rows = []
    for j in range(groups):
        row = misc[j * per, groups : groups + 1, :]
        for i in range(1, per):
            row = row + misc[j * per + i, groups : groups + 1, :]
        county_rows.append(row)
    county_table = jnp.concatenate(county_rows, axis=0)
    n_col = picked(counts, lax.broadcasted_iota(jnp.int32, (n * rows, 1), 0))
    nk_ref[0:1, :] = jnp.broadcast_to(picked(counts, tofc[:, 0:1]), (blocks, LANES)).T[0:1]
    nk_ref[1:2, :] = jnp.broadcast_to(picked(county_table, tofc[:, 0:1]), (blocks, LANES)).T[0:1]
    own_ref[:, 0:1] = n_own
    own_ref[:, 1:2] = picked(county_table, mine_id)

    def spot_of(w):
        return tuple((w >> b) & 1 for b in range(nb - 1, -1, -1))

    def split_into(value_of):
        for w in range(n):
            high, low = halves(value_of(w))
            high_ref[w * rows : (w + 1) * rows, :] = high
            low_ref[w * rows : (w + 1) * rows, :] = low

    def stacked(x, right):
        high, low = halves(x)
        both = product(jnp.concatenate([high, low], axis=0), right)
        return both[: x.shape[0]] + both[x.shape[0] :]

    low_bit = nb - (CHUNKS.bit_length() - 1)
    chunk = me // (1 << low_bit)
    lanes = pl.ds(pl.multiple_of(chunk * LANES, LANES), LANES)
    cov = cover_ref[:, lanes]
    c0, c1, c2, c3 = [cov_ref[l : l + 1, lanes] for l in range(4)]
    v2, v3 = 1.0 / c2, 1.0 / c3
    county_measured = stacked(ca_ref[...] * qp_ref[2:3, :], cov) * v2
    state_row = jnp.broadcast_to(sa_ref[...] * qp_ref[3:4, :], (16, queries))
    state_measured = stacked(state_row, cov)[0:1] * v3
    split_into(lambda w: g1[spot_of(w)])

    for k in range(nb):
        for j in range(parts):
            if j % nb == k:
                tracts_part(j, False)
        if k == 0:
            tbase_ref[...] = stacked(own_sum, cover_ref[...])
        for g in range(2):
            sums[g].wait_recv()
            if k + 1 < nb:
                sums[g] = gather_start(gs, back[g], k + 1, (slice(None), cols[g]))
    split_into(lambda w: gs[spot_of(w)])
    total = two_products(high_ref[...], low_ref[...], cov)
    factor = 1.0 / (n_col * c1 + c0)
    joined = total * factor
    spread = n_col * factor
    jh, jl = halves(joined)
    sh, sl = halves(spread)
    both = jnp.concatenate([jh, jl, sh, sl], axis=1)
    sums4 = jnp.zeros((counties, 4 * LANES), F32)
    for j in range(groups):
        label = lax.broadcasted_iota(jnp.int32, (counties, LANES), 0).astype(F32)
        hot = (label == county_rows[j]).astype(BF16)
        sums4 += product(hot, both[j * LANES : (j + 1) * LANES])
    county_child = sums4[:, :LANES] + sums4[:, LANES : 2 * LANES]
    county_child_spread = sums4[:, 2 * LANES : 3 * LANES] + sums4[:, 3 * LANES :]
    county_total = county_child_spread + v2
    county_joined = (county_child_spread * county_measured + v2 * county_child) / county_total
    county_spread = county_child_spread * v2 / county_total
    state_sum = jnp.sum(county_joined, axis=0, keepdims=True)
    state_spread = jnp.sum(county_spread, axis=0, keepdims=True)
    state_rate = (state_measured - state_sum) / (state_spread + v3)
    spot = at(bit, low_bit)
    g2[spot + (0,)] = (county_measured - county_child + v2 * state_rate) / county_total
    g2[spot + (1,)] = county_joined + county_spread * state_rate
    short = [[b for b in o if b >= low_bit] for o in back]
    last = [gather_start(g2, short[g], 0, (g,), low_bit) for g in range(2)]
    for k in range(len(short[0])):
        for j in range(parts):
            if j % len(short[0]) == k:
                tracts_part(j, True)
        for g in range(2):
            last[g].wait_recv()
            if k + 1 < len(short[0]):
                last[g] = gather_start(g2, short[g], k + 1, (g,), low_bit)
    for c in range(CHUNKS):
        spot = tuple((c >> b) & 1 for b in range(CHUNKS.bit_length() - 2, -1, -1))
        rate_ref[:, c * LANES : (c + 1) * LANES] = g2[spot + (0,)]
        hist_ref[:, c * LANES : (c + 1) * LANES] = g2[spot + (1,)]
    for copy in sends + misc_copies:
        copy.wait_send()


def histogram_kernel(
    base_ref, cov_ref, covt_ref, nk_ref, own_ref, tbase_ref, rate_ref, hist_ref,
    block_ref, tract_ref, county_ref,
):
    counties, width = rate_ref.shape
    blocks = nk_ref.shape[1]
    rows = own_ref.shape[0]
    rate = jnp.concatenate([rate_ref[...], jnp.zeros((LANES - counties, width), F32)], axis=0)
    rh, rl = halves(rate.T)
    label = lax.broadcasted_iota(jnp.int32, (LANES, blocks), 0).astype(F32)
    hot = (label == nk_ref[1:2, :]).astype(BF16)
    above = two_products(rh, rl, hot)
    c0, c1 = covt_ref[:, 0:1], covt_ref[:, 1:2]
    block_ref[...] = base_ref[...] + above / (nk_ref[0:1, :] * c1 + c0)

    label = lax.broadcasted_iota(jnp.int32, (rows, LANES), 1).astype(F32)
    hot = (label == own_ref[:, 1:2]).astype(BF16)
    rh, rl = halves(rate)
    n_own = own_ref[:, 0:1]
    above = product(hot, rh) + product(hot, rl)
    tract_ref[...] = (tbase_ref[...] + n_own * above) / (n_own * cov_ref[1:2, :] + cov_ref[0:1, :])
    county_ref[...] = hist_ref[...]


def local(
    block_answers,
    block_owner,
    block_place,
    tract_answers,
    tract_county,
    county_answers,
    state_answers,
    query_members,
    query_precision,
):
    n = lax.axis_size("wide")
    nb = n.bit_length() - 1
    blocks, queries = block_answers.shape
    rows = tract_answers.shape[0]
    tracts = rows * n
    cells = query_members.shape[0]
    counties = county_answers.shape[0]
    padded = CHUNKS * LANES
    groups = tracts // LANES
    half = queries // 2
    vmem = pl.BlockSpec(memory_space=pltpu.VMEM)
    binary = (2,) * nb
    copies = 8 * nb
    shape = jax.ShapeDtypeStruct
    rbufs = [
        pltpu.VMEM((2,) * (nb - k - 1) + (rows, half), F32) for _ in range(2) for k in range(nb)
    ]
    outs = pl.pallas_call(
        functools.partial(tree_kernel, n),
        out_shape=[
            shape((padded, blocks), F32),
            shape((8, padded), F32),
            shape((padded, LANES), F32),
            shape((8, blocks), F32),
            shape((rows, LANES), F32),
            shape((rows, padded), F32),
            shape((counties, padded), F32),
            shape((counties, padded), F32),
        ],
        in_specs=[vmem] * 9,
        out_specs=[vmem] * 8,
        scratch_shapes=[
            pltpu.VMEM(binary + (rows, queries), F32),
            pltpu.VMEM(binary + (rows, queries), F32),
            pltpu.VMEM(binary + (rows, queries), F32),
            pltpu.VMEM((2,) * (CHUNKS.bit_length() - 1) + (2, counties, LANES), F32),
            pltpu.VMEM((n, groups + 8, LANES), F32),
            pltpu.VMEM((query_members.shape[1], padded), jnp.int32),
            pltpu.VMEM((queries, padded), BF16),
            pltpu.VMEM((padded, queries), BF16),
            pltpu.VMEM((blocks, LANES), jnp.int32),
            pltpu.VMEM((tracts, queries), BF16),
            pltpu.VMEM((tracts, queries), BF16),
            pltpu.SemaphoreType.DMA((n,)),
            pltpu.SemaphoreType.DMA((n,)),
            pltpu.SemaphoreType.DMA((copies,)),
            pltpu.SemaphoreType.DMA((copies,)),
        ]
        + rbufs,
        compiler_params=pltpu.CompilerParams(
            collective_id=0, has_side_effects=True, vmem_limit_bytes=56 * 1024 * 1024
        ),
        name="tree",
    )(
        block_answers,
        block_owner.T,
        block_place[None, :],
        tract_answers,
        tract_county[None, :],
        county_answers,
        state_answers,
        query_members.T,
        query_precision,
    )

    tile = 256
    down = lambda a: pl.BlockSpec((tile, a.shape[1]), lambda i: (i, 0))
    across = lambda a: pl.BlockSpec((a.shape[0], tile), lambda i: (0, i))
    whole = lambda a: pl.BlockSpec(a.shape, lambda i: (0, 0))
    kinds = [down, across, down, whole, whole, across, across, across]
    block_histogram, tract_histogram, county_histogram = pl.pallas_call(
        histogram_kernel,
        grid=(padded // tile,),
        out_shape=[
            shape((cells, blocks), F32),
            shape((rows, cells), F32),
            shape((counties, cells), F32),
        ],
        in_specs=[kind(a) for kind, a in zip(kinds, outs)],
        out_specs=[
            pl.BlockSpec((tile, blocks), lambda i: (i, 0)),
            pl.BlockSpec((rows, tile), lambda i: (0, i)),
            pl.BlockSpec((counties, tile), lambda i: (0, i)),
        ],
        compiler_params=pltpu.CompilerParams(vmem_limit_bytes=56 * 1024 * 1024),
        name="histograms",
    )(*outs)
    return block_histogram.T, tract_histogram, county_histogram


def solution(mesh):
    in_specs = (
        P(("state", "wide"), None),
        P(("state", "wide"), None),
        P(("state", "wide")),
        P(("state", "wide"), None),
        P(("state", "wide")),
        P("state", None),
        P("state", None),
        P(),
        P(),
    )
    out_specs = (P(("state", "wide"), None), P(("state", "wide"), None), P("state", None))
    return jax.shard_map(local, mesh=mesh, in_specs=in_specs, out_specs=out_specs, check_vma=False)
```

```python
import functools
import itertools

import jax
import jax.numpy as jnp
from jax import lax
from jax.experimental import pallas as pl
from jax.experimental.pallas import tpu as pltpu
from jax.sharding import PartitionSpec as P

LANES = 128
CHUNKS = 16
MESH = pl.DeviceIdType.MESH
F32 = jnp.float32
BF16 = jnp.bfloat16


def halves(x):
    high = x.astype(BF16)
    return high, (x - high.astype(F32)).astype(BF16)


def product(left, right):
    return jnp.dot(left, right, preferred_element_type=F32)


def two_products(high, low, right):
    return product(high, right) + product(low, right)


def picked(table, row_of):
    groups = table.shape[0]
    count = row_of.shape[0]
    wide = jnp.zeros((count, LANES), F32)
    for g in range(groups):
        wide = jnp.where(row_of // LANES == g, table[g : g + 1, :], wide)
    lane = lax.broadcasted_iota(jnp.int32, (count, LANES), 1)
    return jnp.sum(jnp.where(lane == row_of % LANES, wide, 0.0), axis=1, keepdims=True)


def nt_product(left, right):
    return lax.dot_general(left, right, (((1,), (1,)), ((), ())), preferred_element_type=F32)


def tree_kernel(
    n,
    ba_ref,
    owner_ref,
    place_ref,
    ta_ref,
    tc_ref,
    ca_ref,
    sa_ref,
    mt_ref,
    qp_ref,
    base_ref,
    cov_ref,
    covt_ref,
    nk_ref,
    own_ref,
    tbase_ref,
    rate_ref,
    hist_ref,
    acc,
    g1,
    gs,
    g2,
    misc,
    mpad,
    cover_ref,
    covert_ref,
    tofc,
    high_ref,
    low_ref,
    misc_send,
    misc_recv,
    send_sems,
    recv_sems,
    *rbufs,
):
    nb = n.bit_length() - 1
    me = lax.axis_index("wide")
    rows, queries = ta_ref.shape
    blocks = ba_ref.shape[0]
    cells = cover_ref.shape[1]
    groups = n * rows // LANES
    counties = rate_ref.shape[0]
    tile = 256
    tall = 512
    half = queries // 2
    bit = [(me // (1 << b)) % 2 for b in range(nb)]
    orders = [list(range(nb)), [0] + list(range(2, nb)) + [1]]
    cols = [pl.ds(0, half), pl.ds(half, half)]
    used = [0]
    sends = []

    def partner(b):
        return me + (1 - 2 * bit[b]) * (1 << b)

    def remote(src, dst, b):
        k = used[0]
        used[0] += 1
        copy = pltpu.make_async_remote_copy(
            src_ref=src,
            dst_ref=dst,
            send_sem=send_sems.at[k],
            recv_sem=recv_sems.at[k],
            device_id={"wide": partner(b)},
            device_id_type=MESH,
        )
        copy.start()
        sends.append(copy)
        return copy

    def at(values, low=0):
        return tuple(values[b] for b in range(nb - 1, low - 1, -1))

    def scatter_start(g, k):
        order = orders[g]
        values = [slice(None)] * nb
        for b in order[:k]:
            values[b] = bit[b]
        values[order[k]] = 1 - bit[order[k]]
        src = acc.at[at(values) + (slice(None), cols[g])]
        return remote(src, rbufs[g * nb + k], order[k])

    def scatter_add(g, k):
        order = orders[g]
        rest = sorted(order[k + 1 :], reverse=True)
        for combo in itertools.product((0, 1), repeat=len(rest)):
            values = list(bit)
            for b, v in zip(rest, combo):
                values[b] = v
            spot = at(values) + (slice(None), cols[g])
            acc[spot] = acc[spot] + rbufs[g * nb + k][combo + (slice(None), slice(None))]

    def gather_start(buf, order, k, tail, low=0):
        values = list(bit)
        for b in order[:k]:
            values[b] = slice(None)
        ref = buf.at[at(values, low) + tail]
        return remote(ref, ref, order[k])

    barrier = pltpu.get_barrier_semaphore()
    for k in range(1, n):
        pl.semaphore_signal(
            barrier, inc=1, device_id={"wide": lax.rem(me + k, n)}, device_id_type=MESH
        )
    pl.semaphore_wait(barrier, n - 1)

    back = [list(reversed(o)) for o in orders]
    g1[at(bit)] = ta_ref[...] * qp_ref[1:2, :]
    tract_copies = [gather_start(g1, back[g], 0, (slice(None), cols[g])) for g in range(2)]

    tof_row = owner_ref[...] * rows + place_ref[...]
    tofc[...] = jnp.broadcast_to(tof_row.astype(F32), (LANES, blocks)).T.astype(jnp.int32)
    tof_col = tofc[:, 0:1]
    row_hot = (lax.broadcasted_iota(jnp.int32, (groups, blocks), 0) == tof_row // LANES).astype(BF16)
    col_hot = (lax.broadcasted_iota(jnp.int32, (blocks, LANES), 1) == tof_col % LANES).astype(BF16)
    misc[me, :groups, :] = product(row_hot, col_hot)
    lane = lax.broadcasted_iota(jnp.int32, (8, LANES), 1)
    mine = lane // rows == me % (LANES // rows)
    misc[me, groups:, :] = jnp.where(mine, jnp.concatenate([tc_ref[...].astype(F32)] * (LANES // rows), axis=1), 0.0)
    misc_copies = []
    for k in range(1, n):
        copy = pltpu.make_async_remote_copy(
            src_ref=misc.at[me],
            dst_ref=misc.at[me],
            send_sem=misc_send.at[k],
            recv_sem=misc_recv.at[k],
            device_id={"wide": lax.rem(me + k, n)},
            device_id_type=MESH,
        )
        copy.start()
        misc_copies.append(copy)

    xh, xl = halves(ba_ref[...] * qp_ref[0:1, :])
    step = min(4, n)
    for c in range(n // step):
        label = lax.broadcasted_iota(jnp.int32, (step * rows, blocks), 0) + c * step * rows
        hot = (label == tof_row).astype(BF16)
        part = product(hot, xh) + product(hot, xl)
        for s in range(step):
            w = c * step + s
            spot = tuple((w >> b) & 1 for b in range(nb - 1, -1, -1))
            acc[spot] = part[s * rows : (s + 1) * rows]

    def tract_step(k):
        for g in range(2):
            tract_copies[g].wait_recv()
            if k + 1 < nb:
                tract_copies[g] = gather_start(g1, back[g], k + 1, (slice(None), cols[g]))

    tract_step(0)
    sums = [scatter_start(g, 0) for g in range(2)]

    def scatter_step(k):
        for g in range(2):
            sums[g].wait_recv()
            scatter_add(g, k)
            if k + 1 < nb:
                sums[g] = scatter_start(g, k + 1)

    scatter_step(0)
    tract_step(1)

    mpad[...] = jnp.zeros_like(mpad)
    mpad[:, : mt_ref.shape[1]] = mt_ref[...]

    def cover_lanes(i, carry):
        spot = pl.ds(pl.multiple_of(i * LANES, LANES), LANES)
        label = lax.broadcasted_iota(jnp.int32, (queries, LANES), 0)
        total = jnp.zeros((queries, LANES), F32)
        for m in range(mpad.shape[0]):
            total = total + jnp.where(label == mpad[m : m + 1, spot], 1.0, 0.0)
        cover_ref[:, spot] = total.astype(BF16)
        covert_ref[spot, :] = total.T.astype(BF16)
        return carry

    lax.fori_loop(0, cells // LANES, cover_lanes, 0)
    weights = jnp.concatenate([qp_ref[...], qp_ref[...]], axis=0)
    w0, _ = halves(weights)
    w1, w2 = halves(weights - w0.astype(F32))
    cover = cover_ref[...]
    coverage = product(w0, cover) + product(w1, cover) + product(w2, cover)
    cov_ref[...] = coverage
    blank = jnp.zeros((LANES - 8, LANES), F32)
    for c in range(cells // LANES):
        piece = slice(c * LANES, (c + 1) * LANES)
        covt_ref[piece, :] = jnp.concatenate([coverage[:, piece], blank], axis=0).T

    def tracts_part(j, of_sums):
        spot = slice(j * tile, (j + 1) * tile)
        label = lax.broadcasted_iota(jnp.int32, (tile, n * rows), 1)
        hot = (label == tofc[spot, 0:1]).astype(BF16)
        ph = product(hot, high_ref[...]).astype(BF16)
        pl_ = product(hot, low_ref[...]).astype(BF16)
        n_row = nk_ref[0:1, spot]
        if not of_sums:
            near = ph.astype(F32) + pl_.astype(F32) + ba_ref[spot, :] * qp_ref[0:1, :]
            ph, pl_ = halves(near)

        def body(i, carry):
            down = pl.ds(pl.multiple_of(i * tall, tall), tall)
            left = covert_ref[down, :]
            total = nt_product(left, ph) + nt_product(left, pl_)
            c0, c1 = covt_ref[down, 0:1], covt_ref[down, 1:2]
            if of_sums:
                scaled = total * (c1 / c0) / (n_row * c1 + c0)
                base_ref[down, spot] = base_ref[down, spot] - scaled
            else:
                base_ref[down, spot] = total * (1.0 / c0)
            return carry

        lax.fori_loop(0, cells // tall, body, 0)

    parts = blocks // tile
    for copy in misc_copies:
        copy.wait_recv()
    counts = misc[0, :groups, :]
    for d in range(1, n):
        counts = counts + misc[d, :groups, :]
    mine_id = lax.broadcasted_iota(jnp.int32, (rows, 1), 0) + me * rows
    n_own = picked(counts, mine_id)
    for k in range(1, nb):
        scatter_step(k)
        if 1 < k < nb - 1:
            tract_step(k)

    own_sum = n_own * (ta_ref[...] * qp_ref[1:2, :]) + acc[at(bit)]
    gs[at(bit)] = own_sum
    sums = [gather_start(gs, back[g], 0, (slice(None), cols[g])) for g in range(2)]
    tract_step(nb - 1)

    per = LANES // rows
    county_rows = []
    for j in range(groups):
        row = misc[j * per, groups : groups + 1, :]
        for i in range(1, per):
            row = row + misc[j * per + i, groups : groups + 1, :]
        county_rows.append(row)
    county_table = jnp.concatenate(county_rows, axis=0)
    n_col = picked(counts, lax.broadcasted_iota(jnp.int32, (n * rows, 1), 0))
    nk_ref[0:1, :] = jnp.broadcast_to(picked(counts, tofc[:, 0:1]), (blocks, LANES)).T[0:1]
    nk_ref[1:2, :] = jnp.broadcast_to(picked(county_table, tofc[:, 0:1]), (blocks, LANES)).T[0:1]
    own_ref[:, 0:1] = n_own
    own_ref[:, 1:2] = picked(county_table, mine_id)

    def spot_of(w):
        return tuple((w >> b) & 1 for b in range(nb - 1, -1, -1))

    def split_into(value_of):
        for w in range(n):
            high, low = halves(value_of(w))
            high_ref[w * rows : (w + 1) * rows, :] = high
            low_ref[w * rows : (w + 1) * rows, :] = low

    def stacked(x, right):
        high, low = halves(x)
        both = product(jnp.concatenate([high, low], axis=0), right)
        return both[: x.shape[0]] + both[x.shape[0] :]

    low_bit = nb - (CHUNKS.bit_length() - 1)
    chunk = me // (1 << low_bit)
    lanes = pl.ds(pl.multiple_of(chunk * LANES, LANES), LANES)
    cov = cover_ref[:, lanes]
    c0, c1, c2, c3 = [cov_ref[l : l + 1, lanes] for l in range(4)]
    v2, v3 = 1.0 / c2, 1.0 / c3
    county_measured = stacked(ca_ref[...] * qp_ref[2:3, :], cov) * v2
    state_row = jnp.broadcast_to(sa_ref[...] * qp_ref[3:4, :], (16, queries))
    state_measured = stacked(state_row, cov)[0:1] * v3
    split_into(lambda w: g1[spot_of(w)])

    for k in range(nb):
        for j in range(parts):
            if j % nb == k:
                tracts_part(j, False)
        if k == 0:
            tbase_ref[...] = stacked(own_sum, cover_ref[...])
        for g in range(2):
            sums[g].wait_recv()
            if k + 1 < nb:
                sums[g] = gather_start(gs, back[g], k + 1, (slice(None), cols[g]))
    split_into(lambda w: gs[spot_of(w)])
    total = two_products(high_ref[...], low_ref[...], cov)
    factor = 1.0 / (n_col * c1 + c0)
    joined = total * factor
    spread = n_col * factor
    jh, jl = halves(joined)
    sh, sl = halves(spread)
    both = jnp.concatenate([jh, jl, sh, sl], axis=1)
    sums4 = jnp.zeros((counties, 4 * LANES), F32)
    for j in range(groups):
        label = lax.broadcasted_iota(jnp.int32, (counties, LANES), 0).astype(F32)
        hot = (label == county_rows[j]).astype(BF16)
        sums4 += product(hot, both[j * LANES : (j + 1) * LANES])
    county_child = sums4[:, :LANES] + sums4[:, LANES : 2 * LANES]
    county_child_spread = sums4[:, 2 * LANES : 3 * LANES] + sums4[:, 3 * LANES :]
    county_total = county_child_spread + v2
    county_joined = (county_child_spread * county_measured + v2 * county_child) / county_total
    county_spread = county_child_spread * v2 / county_total
    state_sum = jnp.sum(county_joined, axis=0, keepdims=True)
    state_spread = jnp.sum(county_spread, axis=0, keepdims=True)
    state_rate = (state_measured - state_sum) / (state_spread + v3)
    spot = at(bit, low_bit)
    g2[spot + (0,)] = (county_measured - county_child + v2 * state_rate) / county_total
    g2[spot + (1,)] = county_joined + county_spread * state_rate
    short = [[b for b in o if b >= low_bit] for o in back]
    last = [gather_start(g2, short[g], 0, (g,), low_bit) for g in range(2)]
    for k in range(len(short[0])):
        for j in range(parts):
            if j % len(short[0]) == k:
                tracts_part(j, True)
        for g in range(2):
            last[g].wait_recv()
            if k + 1 < len(short[0]):
                last[g] = gather_start(g2, short[g], k + 1, (g,), low_bit)
    for c in range(CHUNKS):
        spot = tuple((c >> b) & 1 for b in range(CHUNKS.bit_length() - 2, -1, -1))
        rate_ref[:, c * LANES : (c + 1) * LANES] = g2[spot + (0,)]
        hist_ref[:, c * LANES : (c + 1) * LANES] = g2[spot + (1,)]
    for copy in sends + misc_copies:
        copy.wait_send()


def histogram_kernel(
    base_ref, cov_ref, covt_ref, nk_ref, own_ref, tbase_ref, rate_ref, hist_ref,
    block_ref, tract_ref, county_ref,
):
    counties, width = rate_ref.shape
    blocks = nk_ref.shape[1]
    rows = own_ref.shape[0]
    rate = jnp.concatenate([rate_ref[...], jnp.zeros((LANES - counties, width), F32)], axis=0)
    rh, rl = halves(rate.T)
    label = lax.broadcasted_iota(jnp.int32, (LANES, blocks), 0).astype(F32)
    hot = (label == nk_ref[1:2, :]).astype(BF16)
    above = two_products(rh, rl, hot)
    c0, c1 = covt_ref[:, 0:1], covt_ref[:, 1:2]
    block_ref[...] = base_ref[...] + above / (nk_ref[0:1, :] * c1 + c0)

    label = lax.broadcasted_iota(jnp.int32, (rows, LANES), 1).astype(F32)
    hot = (label == own_ref[:, 1:2]).astype(BF16)
    rh, rl = halves(rate)
    n_own = own_ref[:, 0:1]
    above = product(hot, rh) + product(hot, rl)
    tract_ref[...] = (tbase_ref[...] + n_own * above) / (n_own * cov_ref[1:2, :] + cov_ref[0:1, :])
    county_ref[...] = hist_ref[...]


def local(
    block_answers,
    block_owner,
    block_place,
    tract_answers,
    tract_county,
    county_answers,
    state_answers,
    query_members,
    query_precision,
):
    n = lax.axis_size("wide")
    nb = n.bit_length() - 1
    blocks, queries = block_answers.shape
    rows = tract_answers.shape[0]
    tracts = rows * n
    cells = query_members.shape[0]
    counties = county_answers.shape[0]
    padded = CHUNKS * LANES
    groups = tracts // LANES
    half = queries // 2
    vmem = pl.BlockSpec(memory_space=pltpu.VMEM)
    binary = (2,) * nb
    copies = 8 * nb
    shape = jax.ShapeDtypeStruct
    rbufs = [
        pltpu.VMEM((2,) * (nb - k - 1) + (rows, half), F32) for _ in range(2) for k in range(nb)
    ]
    outs = pl.pallas_call(
        functools.partial(tree_kernel, n),
        out_shape=[
            shape((padded, blocks), F32),
            shape((8, padded), F32),
            shape((padded, LANES), F32),
            shape((8, blocks), F32),
            shape((rows, LANES), F32),
            shape((rows, padded), F32),
            shape((counties, padded), F32),
            shape((counties, padded), F32),
        ],
        in_specs=[vmem] * 9,
        out_specs=[vmem] * 8,
        scratch_shapes=[
            pltpu.VMEM(binary + (rows, queries), F32),
            pltpu.VMEM(binary + (rows, queries), F32),
            pltpu.VMEM(binary + (rows, queries), F32),
            pltpu.VMEM((2,) * (CHUNKS.bit_length() - 1) + (2, counties, LANES), F32),
            pltpu.VMEM((n, groups + 8, LANES), F32),
            pltpu.VMEM((query_members.shape[1], padded), jnp.int32),
            pltpu.VMEM((queries, padded), BF16),
            pltpu.VMEM((padded, queries), BF16),
            pltpu.VMEM((blocks, LANES), jnp.int32),
            pltpu.VMEM((tracts, queries), BF16),
            pltpu.VMEM((tracts, queries), BF16),
            pltpu.SemaphoreType.DMA((n,)),
            pltpu.SemaphoreType.DMA((n,)),
            pltpu.SemaphoreType.DMA((copies,)),
            pltpu.SemaphoreType.DMA((copies,)),
        ]
        + rbufs,
        compiler_params=pltpu.CompilerParams(
            collective_id=0, has_side_effects=True, vmem_limit_bytes=56 * 1024 * 1024
        ),
        name="tree",
    )(
        block_answers,
        block_owner.T,
        block_place[None, :],
        tract_answers,
        tract_county[None, :],
        county_answers,
        state_answers,
        query_members.T,
        query_precision,
    )

    tile = 256
    down = lambda a: pl.BlockSpec((tile, a.shape[1]), lambda i: (i, 0))
    across = lambda a: pl.BlockSpec((a.shape[0], tile), lambda i: (0, i))
    whole = lambda a: pl.BlockSpec(a.shape, lambda i: (0, 0))
    kinds = [down, across, down, whole, whole, across, across, across]
    block_histogram, tract_histogram, county_histogram = pl.pallas_call(
        histogram_kernel,
        grid=(padded // tile,),
        out_shape=[
            shape((cells, blocks), F32),
            shape((rows, cells), F32),
            shape((counties, cells), F32),
        ],
        in_specs=[kind(a) for kind, a in zip(kinds, outs)],
        out_specs=[
            pl.BlockSpec((tile, blocks), lambda i: (i, 0)),
            pl.BlockSpec((rows, tile), lambda i: (0, i)),
            pl.BlockSpec((counties, tile), lambda i: (0, i)),
        ],
        compiler_params=pltpu.CompilerParams(vmem_limit_bytes=56 * 1024 * 1024),
        name="histograms",
    )(*outs)
    return block_histogram.T, tract_histogram, county_histogram


def solution(mesh):
    in_specs = (
        P(("state", "wide"), None),
        P(("state", "wide"), None),
        P(("state", "wide")),
        P(("state", "wide"), None),
        P(("state", "wide")),
        P("state", None),
        P("state", None),
        P(),
        P(),
    )
    out_specs = (P(("state", "wide"), None), P(("state", "wide"), None), P("state", None))
    return jax.shard_map(local, mesh=mesh, in_specs=in_specs, out_specs=out_specs, check_vma=False)
```
